32 devices in a mesh: req: 4 (over y, core), exp: 8 (over z, x).
Axes of the slice: x: 2, y: 2, z: 4, core: 2. Of those that a mesh axis runs over, the one named last changes fastest.
Arguments:
- queries: bfloat16 [64, 64, 2048], P('req', None, 'exp'), may hold values from -42 to 42
- new_keys: bfloat16 [64, 64, 2048], P('req', None, 'exp'), may hold values from -6 to 6
- new_values: bfloat16 [64, 64, 2048], P('req', None, 'exp'), may hold values from -6 to 6
- long_keys: bfloat16 [4, 16384, 2048], P('req', None, 'exp'), may hold values from -18 to 18
- long_values: bfloat16 [4, 16384, 2048], P('req', None, 'exp'), may hold values from -6 to 6
- long_lengths: int32 [4], P('req'), may hold values from 4096 to 16384
- short_keys: bfloat16 [60, 1024, 2048], P('req', None, 'exp'), may hold values from -18 to 18
- short_values: bfloat16 [60, 1024, 2048], P('req', None, 'exp'), may hold values from -6 to 6
- short_lengths: int32 [60], P('req'), may hold values from 256 to 1024
- parents: int32 [64, 64], P('req'), may hold values from 0 to 62, as said below
- accepted: int32 [64], P('req'), may hold values from 0 to 63
- residual: float32 [4096, 2048], P(('req', 'exp')), may hold values from -18 to 18
- out_weight: bfloat16 [2048, 2048], P('exp'), may hold values from -2 to 2
- norm_gain: float32 [2048], replicated, may hold values from 0.5 to 1.5
- routes: int32 [4096, 8], P(('req', 'exp')), may hold values from 0 to 63, all different within a row; in each aligned block of 128 rows (0 to 127, 128 to 255, ...) at most 32 rows name the same one
- route_weights: float32 [4096, 8], P(('req', 'exp')), may hold values from 0.05 to 0.4
- expert_gate: bfloat16 [64, 2048, 1024], P(('req', 'exp')), may hold values from -0.125 to 0.125
- expert_up: bfloat16 [64, 2048, 1024], P(('req', 'exp')), may hold values from -0.125 to 0.125
- expert_down: bfloat16 [64, 1024, 2048], P(('req', 'exp')), may hold values from -0.1875 to 0.1875
Outputs:
- hidden_out: bfloat16 [4096, 2048], P(('req', 'exp'))
- accepted_keys: bfloat16 [64, 64, 2048], P('req', None, 'exp')
- accepted_values: bfloat16 [64, 64, 2048], P('req', None, 'exp')
The draws below stay inside these ranges and needn't reach their ends.
Inputs may be any that keep to these rules, and one draw needn't show every extreme that they name: parents[r, 0] = 0 (the root); for t >= 1, parents[r, t] < t. `routes`: each row names 8 different experts; within the 128 rows of one device (aligned blocks) no expert is named by more than 32 rows.
All inputs are finite; a program needn't handle non-finite values.
Results may differ from the reference program's by a relative error of at most 0.02.
Values may be sent and summed in bfloat16 or wider, within the bound.
A program may use at most 128 MiB of HBM per device.

```python
import math
import jax
import jax.numpy as jnp
import numpy as np
from jax import lax

D = 2048
HEAD = 128
FF = 1024
EXPERTS = 64
TOPK = 8
DRAFT = 64
LMAX = 16384
SMAX = 1024
SHORT_DEV = 15
HD = 2048
REQ_DEV = 16
LONG = 4
SHORT = 60
REQS = 64
TOKENS = 4096
TOK_DEV = 128
PIECES = 1
FF_DEV = 1024
SLICES = 64
CAP = 32
N_REQ = 4
N_EXP = 8


def first_rows(key, number):
    return jax.random.truncated_normal(jax.random.fold_in(key, 1), -6.0, 6.0, (number, 1, HD), jnp.float32)


def cache_rows(key, number, positions):
    first = first_rows(key, number)
    others = jax.random.truncated_normal(jax.random.fold_in(key, 2), -6.0, 6.0, (number, positions - 1, HD), jnp.float32)
    return jnp.concatenate([first, others], axis=1)


def draw_long_keys(key, part):
    return cache_rows(jax.random.fold_in(key, 101), LONG, LMAX).astype(jnp.bfloat16)


def draw_short_keys(key, part):
    return cache_rows(jax.random.fold_in(key, 102), SHORT, SMAX).astype(jnp.bfloat16)


def draw_queries(key, part):
    base = jax.random.truncated_normal(jax.random.fold_in(key, 103), -6.0, 6.0, (REQS, DRAFT, HD), jnp.float32)
    return base.astype(jnp.bfloat16)


def draw_long_lengths(key, part):
    drawn = jax.random.randint(jax.random.fold_in(key, 104), (LONG,), LMAX // 4, LMAX + 1, dtype=jnp.int32)
    return jnp.where(jnp.arange(LONG, dtype=jnp.int32) == 0, LMAX, drawn).astype(jnp.int32)


def draw_short_lengths(key, part):
    drawn = jax.random.randint(jax.random.fold_in(key, 105), (SHORT,), SMAX // 4, SMAX + 1, dtype=jnp.int32)
    return jnp.where(jnp.arange(SHORT, dtype=jnp.int32) == 0, SMAX, drawn).astype(jnp.int32)


def draw_parents(key, part):
    position = jnp.arange(DRAFT, dtype=jnp.int32)
    upper = jnp.broadcast_to(jnp.maximum(position, 1)[None, :], (REQS, DRAFT))
    drawn = jax.random.randint(jax.random.fold_in(key, 106), (REQS, DRAFT), 0, upper, dtype=jnp.int32)
    request = jnp.arange(REQS, dtype=jnp.int32)
    pinned = (request[:, None] == 0) & (position[None, :] == DRAFT - 1)
    return jnp.where(pinned, DRAFT - 2, drawn).astype(jnp.int32)


def draw_residual(key, part):
    row_scale = jnp.exp(jax.random.uniform(jax.random.fold_in(key, 107), (TOKENS, 1), jnp.float32, math.log(0.1), 0.0))
    col_scale = jnp.exp(jax.random.uniform(jax.random.fold_in(key, 108), (1, D), jnp.float32, math.log(0.3), math.log(3.0)))
    noise = jax.random.truncated_normal(jax.random.fold_in(key, 110), -6.0, 6.0, (TOKENS, D), jnp.float32)
    return noise * row_scale * col_scale


def touch_ends(values, own_key, low, high):
    extent = values.shape
    place = [jax.random.randint(jax.random.fold_in(own_key, axis), (), 0, extent[axis]) for axis in range(len(extent))]
    values = values.at[tuple(place)].set(low)
    longest = extent.index(max(extent))
    place[longest] = (place[longest] + 1) % extent[longest]
    return values.at[tuple(place)].set(high)


def level_of(own_key, dims, split, smallest, high):
    gain, own = 1.0, jax.random.fold_in(own_key, 6)
    for dim, parts in split:
        heights = jnp.exp(jax.random.uniform(jax.random.fold_in(own, dim), (parts,), jnp.float32, smallest / len(split), high / len(split)))
        gain = gain * jnp.repeat(heights, dims[dim] // parts).reshape([-1 if axis == dim else 1 for axis in range(len(dims))])
    return gain


def routed_block(key, own, number, rows, amount, top, limit, slope):
    ranking = jax.random.permutation(key, amount)
    crowded, usual = shares(amount, rows * top, limit, slope, True), shares(amount, rows * top, limit, slope, False)
    places = jnp.arange(amount)

    def named(sizes, offset_by):
        used = int((sizes > 0).sum())
        fixed = max(1, used // 4)
        moved = fixed + (places - fixed + offset_by * (used - fixed)) % max(1, amount - fixed)
        return jnp.zeros((amount,), jnp.int32).at[ranking[jnp.where(places < fixed, places, moved)]].set(jnp.asarray(sizes, jnp.int32))

    sizes = jnp.where(number % 4 == 0, named(crowded, number // 4), named(usual, number - number // 4 - 1))
    mixed = jax.random.permutation(jax.random.fold_in(own, 3), amount)
    donor, taker = mixed[0:amount // 2 * 2:2], mixed[1:amount // 2 * 2:2]
    slack = jnp.minimum(sizes[donor] - 1, limit - sizes[taker]) // 2
    slack = jnp.where((donor == ranking[0]) | (taker == ranking[0]) | (sizes[taker] == 0), 0, jnp.maximum(slack, 0))
    moved = jax.random.randint(jax.random.fold_in(own, 4), (amount // 2,), 0, 1 << 20) % (slack + 1)
    sizes = sizes.at[donor].add(-moved).at[taker].add(moved)
    labels = jnp.searchsorted(jnp.cumsum(sizes), jnp.arange(rows * top), side="right").astype(jnp.int32)
    grid = labels.reshape(top, rows).T
    grid = grid[jax.random.permutation(jax.random.fold_in(own, 1), rows)]
    offset_by = jax.random.randint(jax.random.fold_in(own, 2), (rows, 1), 0, top)
    return jnp.take_along_axis(grid, (jnp.arange(top)[None, :] + offset_by) % top, axis=1)


def shares(count, total, reach, lean, full):
    weights = [(1 << 20) // math.isqrt(standing ** lean) + 1 for standing in range(1, count + 1)]
    largest = reach if full else min(reach, max(-(-total // count), total * weights[0] // sum(weights)))
    least = 1 if total - largest >= count - 1 else 0
    counts, rest = [largest] + [least] * (count - 1), total - largest - least * (count - 1)
    while rest > 0:
        movable = [i for i in range(1, count) if counts[i] < largest] or [i for i in range(1, count) if counts[i] < reach]
        whole, budget = sum([weights[i] for i in movable]), rest
        for i in movable:
            more = min(reach - counts[i], max(1, budget * weights[i] // whole), rest)
            counts[i] = counts[i] + more
            rest = rest - more
    return np.array(counts)


def normal_values(own_key, extent, deviation, most, cuts=(), kind=jnp.bfloat16):
    values = jax.random.normal(own_key, extent, jnp.float32) * deviation
    if len(cuts) > 0:
        values = level_of(own_key, extent, cuts, -0.22, 0.18) * values
    return jnp.clip(values, min=-most, max=most).astype(kind)


def setup_inputs(seed: int = 0) -> dict:
    key_of = jax.random.split(jax.random.key(seed), 20)
    queries = draw_queries(jax.random.fold_in(key_of[19], 71), 0)
    new_keys = normal_values(key_of[1], (REQS, DRAFT, HD), 1.0, 6.0, ((0, 4), (2, 8)))
    new_values = normal_values(key_of[2], (REQS, DRAFT, HD), 1.0, 6.0, ((0, 4), (2, 8)))
    long_keys = draw_long_keys(jax.random.fold_in(key_of[19], 71), 0)
    long_values = normal_values(key_of[4], (LONG, LMAX, HD), 1.0, 6.0, ((0, 4), (2, 8)))
    long_lengths = draw_long_lengths(jax.random.fold_in(key_of[19], 71), 0)
    short_keys = draw_short_keys(jax.random.fold_in(key_of[19], 71), 0)
    short_values = normal_values(key_of[7], (SHORT, SMAX, HD), 1.0, 6.0, ((0, 4), (2, 8)))
    short_lengths = draw_short_lengths(jax.random.fold_in(key_of[19], 71), 0)
    parents = draw_parents(jax.random.fold_in(key_of[19], 71), 0)
    accepted = touch_ends(jax.random.randint(key_of[10], (REQS,), 0, DRAFT), jax.random.fold_in(key_of[10], 1), 0, DRAFT - 1).astype(jnp.int32)
    residual = draw_residual(jax.random.fold_in(key_of[19], 71), 0)
    out_weight = normal_values(key_of[12], (HD, D), 8 ** -0.5, 2.0, ((0, 8),))
    norm_gain = jnp.clip(1.0 + 0.1 * jax.random.normal(key_of[13], (D,), jnp.float32), 0.5, 1.5)
    routes_keys = jax.random.split(jax.random.fold_in(key_of[14], 1), TOKENS // TOK_DEV)
    routes_turns = jax.random.permutation(jax.random.fold_in(key_of[14], 3), TOKENS // TOK_DEV)
    routes = jax.vmap(lambda own, number: routed_block(jax.random.fold_in(key_of[14], 2), own, number, TOK_DEV, EXPERTS, TOPK, CAP, 2))(routes_keys, routes_turns).reshape((TOKENS, TOPK))
    route_weights = jnp.clip(0.05 + 0.35 * jax.random.uniform(key_of[15], (TOKENS, TOPK), jnp.float32) ** level_of(key_of[15], (TOKENS, TOPK), ((0, 32),), -0.2, 0.2), 0.05, 0.4)
    expert_gate = normal_values(key_of[16], (SLICES, D, FF_DEV), D ** -0.5, 0.125, ((0, 32),))
    expert_up = normal_values(key_of[17], (SLICES, D, FF_DEV), D ** -0.5, 0.125, ((0, 32),))
    expert_down = normal_values(key_of[18], (SLICES, FF_DEV, D), FF ** -0.5, 0.1875, ((0, 32),))
    return {"queries": queries, "new_keys": new_keys, "new_values": new_values, "long_keys": long_keys, "long_values": long_values, "long_lengths": long_lengths, "short_keys": short_keys, "short_values": short_values, "short_lengths": short_lengths, "parents": parents, "accepted": accepted, "residual": residual, "out_weight": out_weight, "norm_gain": norm_gain, "routes": routes, "route_weights": route_weights, "expert_gate": expert_gate, "expert_up": expert_up, "expert_down": expert_down}


def ancestors(parents):
    tokens_per = parents.shape[1]
    position = jnp.arange(tokens_per, dtype=jnp.int32)
    identity = (position[:, None] == position[None, :]).astype(jnp.float32)
    linked = (parents[:, :, None] == position[None, None, :]) & (position[None, :, None] > 0)
    reached = jnp.maximum(identity[None], linked.astype(jnp.float32))
    for rounds in range(tokens_per.bit_length()):
        reached = jnp.minimum(jnp.einsum('bij,bjk->bik', reached, reached, precision=lax.Precision.HIGHEST), 1.0)
    return reached

def compact_path(reached, accepted, stacked):
    tokens_per = reached.shape[1]
    position = jnp.arange(tokens_per, dtype=jnp.int32)
    levels = lax.optimization_barrier(jnp.sum(reached, axis=2)) - 1.0
    leaf_row = (accepted[:, None] == position[None, :]).astype(jnp.float32)
    on_path = jnp.einsum('bi,bij->bj', leaf_row, reached, precision=lax.Precision.HIGHEST)
    chooser = on_path[:, None, :] * (levels[:, None, :] == position[None, :, None].astype(jnp.float32)).astype(jnp.float32)
    return jnp.einsum('btj,bjc->btc', chooser, stacked.astype(jnp.float32), precision=lax.Precision.HIGHEST).astype(jnp.bfloat16)

def attend(queries, cache_keys, cache_values, lengths, new_keys, new_values, reached):
    batch, tokens_per, width = queries.shape
    heads = width // HEAD
    scale = HEAD ** (-0.5)
    shape_q = (batch, tokens_per, heads, HEAD)
    shape_c = (batch, cache_keys.shape[1], heads, HEAD)
    query_four = queries.reshape(shape_q).astype(jnp.float32)
    cache_scores = jnp.einsum('bthe,blhe->bhtl', query_four, cache_keys.reshape(shape_c).astype(jnp.float32)) * scale
    valid = jnp.arange(cache_keys.shape[1], dtype=jnp.int32)[None, :] < lengths[:, None]
    cache_scores = jnp.where(valid[:, None, None, :], cache_scores, -jnp.inf)
    draft_scores = jnp.einsum('bthe,bshe->bhts', query_four, new_keys.reshape(shape_q).astype(jnp.float32)) * scale
    draft_scores = jnp.where(reached[:, None] > 0.5, draft_scores, -jnp.inf)
    highest = jnp.maximum(lax.optimization_barrier(jnp.max(cache_scores, axis=3)), lax.optimization_barrier(jnp.max(draft_scores, axis=3)))
    cache_probs = jnp.exp(cache_scores - highest[..., None])
    draft_probs = jnp.exp(draft_scores - highest[..., None])
    totals = lax.optimization_barrier(jnp.sum(cache_probs, axis=3)) + lax.optimization_barrier(jnp.sum(draft_probs, axis=3))
    cache_round = lax.optimization_barrier(cache_probs.astype(jnp.bfloat16)).astype(jnp.float32)
    draft_round = lax.optimization_barrier(draft_probs.astype(jnp.bfloat16)).astype(jnp.float32)
    mixed = jnp.einsum('bhtl,blhe->bthe', cache_round, cache_values.reshape(shape_c).astype(jnp.float32))
    mixed = mixed + jnp.einsum('bhts,bshe->bthe', draft_round, new_values.reshape(shape_q).astype(jnp.float32))
    mixed = mixed / jnp.transpose(totals, (0, 2, 1))[..., None]
    return mixed.reshape(batch, tokens_per, width).astype(jnp.bfloat16)

def single_request(item):
    return attend(*[member[None] for member in item])[0]

def reference(queries, new_keys, new_values, long_keys, long_values, long_lengths, short_keys, short_values, short_lengths, parents, accepted, residual, out_weight, norm_gain, routes, route_weights, expert_gate, expert_up, expert_down):
    reached = ancestors(parents)
    stacked = jnp.concatenate([new_keys, new_values], axis=2)
    compacted = compact_path(reached, accepted, stacked)
    accepted_keys = compacted[:, :, :HD]
    accepted_values = compacted[:, :, HD:]
    query_groups = queries.reshape(LONG, REQ_DEV, DRAFT, HD)
    key_groups = new_keys.reshape(LONG, REQ_DEV, DRAFT, HD)
    value_groups = new_values.reshape(LONG, REQ_DEV, DRAFT, HD)
    reach_groups = reached.reshape(LONG, REQ_DEV, DRAFT, DRAFT)
    long_items = (query_groups[:, 0], long_keys, long_values, long_lengths, key_groups[:, 0], value_groups[:, 0], reach_groups[:, 0])
    short_items = (query_groups[:, 1:].reshape(SHORT, DRAFT, HD), short_keys, short_values, short_lengths, key_groups[:, 1:].reshape(SHORT, DRAFT, HD), value_groups[:, 1:].reshape(SHORT, DRAFT, HD), reach_groups[:, 1:].reshape(SHORT, DRAFT, DRAFT))
    long_out = lax.map(single_request, long_items)
    short_out = lax.map(single_request, short_items)
    attended = jnp.concatenate([long_out[:, None], short_out.reshape(LONG, SHORT_DEV, DRAFT, HD)], axis=1).reshape(TOKENS, HD)
    attn_proj = jnp.dot(attended, out_weight, preferred_element_type=jnp.float32)
    middle = residual + attn_proj
    normed = (middle * lax.rsqrt(lax.optimization_barrier(jnp.mean(middle * middle, axis=1, keepdims=True)) + 1e-05) * norm_gain).astype(jnp.bfloat16)
    flat_routes = routes.reshape(-1)
    order = jnp.argsort(flat_routes, stable=True).astype(jnp.int32)
    sorted_experts = flat_routes[order]
    token_of = (order // TOPK).astype(jnp.int32)
    weight_of = route_weights.reshape(-1)[order]
    window = CAP * N_REQ * N_EXP
    starts = jnp.searchsorted(sorted_experts, jnp.arange(EXPERTS, dtype=jnp.int32)).astype(jnp.int32)
    token_pad = jnp.concatenate([token_of, jnp.zeros((window,), jnp.int32)])
    expert_pad = jnp.concatenate([sorted_experts, jnp.full((window,), EXPERTS, jnp.int32)])
    weight_pad = jnp.concatenate([weight_of, jnp.zeros((window,), jnp.float32)])

    def one_expert(carry, expert):
        begin = starts[expert]
        rows_index = lax.dynamic_slice_in_dim(token_pad, begin, window)
        owners = lax.dynamic_slice_in_dim(expert_pad, begin, window)
        weights_here = jnp.where(owners == expert, lax.dynamic_slice_in_dim(weight_pad, begin, window), 0.0)
        chosen = normed[rows_index]
        combined = jnp.zeros((window, D), jnp.float32)
        for piece in range(PIECES):
            index = expert * PIECES + piece
            gate_w = lax.dynamic_index_in_dim(expert_gate, index, 0, keepdims=False)
            up_w = lax.dynamic_index_in_dim(expert_up, index, 0, keepdims=False)
            down_w = lax.dynamic_index_in_dim(expert_down, index, 0, keepdims=False)
            gate_part = jnp.dot(chosen, gate_w, preferred_element_type=jnp.float32)
            up_part = jnp.dot(chosen, up_w, preferred_element_type=jnp.float32)
            activation = (jax.nn.silu(gate_part) * up_part).astype(jnp.bfloat16)
            piece_out = jnp.dot(activation, down_w, preferred_element_type=jnp.float32).astype(jnp.bfloat16)
            combined = combined + piece_out.astype(jnp.float32)
        return (carry.at[rows_index].add(weights_here[:, None] * combined), None)
    moe, _ = lax.scan(one_expert, jnp.zeros((TOKENS, D), jnp.float32), jnp.arange(EXPERTS, dtype=jnp.int32))
    hidden_out = (middle + moe).astype(jnp.bfloat16)
    return (hidden_out, accepted_keys, accepted_values)
```

```python
import jax
import jax.numpy as jnp
from jax import lax
from jax.sharding import PartitionSpec as P

HEAD = 128
EXPERTS = 64


def ancestors(parents):
    tokens_per = parents.shape[1]
    position = jnp.arange(tokens_per, dtype=jnp.int32)
    identity = position[:, None] == position[None, :]
    linked = (parents[:, :, None] == position[None, None, :]) & (position[None, :, None] > 0)
    reached = (identity[None] | linked).astype(jnp.bfloat16)
    for rounds in range((tokens_per - 1).bit_length()):
        reached = jnp.minimum(
            jnp.einsum("bij,bjk->bik", reached, reached, preferred_element_type=jnp.float32), 1.0
        ).astype(jnp.bfloat16)
    return reached.astype(jnp.float32)


def compact_path(reached, accepted, stacked):
    tokens_per = reached.shape[1]
    position = jnp.arange(tokens_per, dtype=jnp.int32)
    levels = jnp.sum(reached, axis=2) - 1.0
    leaf_row = (accepted[:, None] == position[None, :]).astype(jnp.float32)
    on_path = jnp.sum(leaf_row[:, :, None] * reached, axis=1)
    chooser = on_path[:, None, :] * (
        levels[:, None, :] == position[None, :, None].astype(jnp.float32)
    ).astype(jnp.float32)
    return jnp.einsum(
        "btj,bjc->btc", chooser.astype(jnp.bfloat16), stacked, preferred_element_type=jnp.float32
    ).astype(jnp.bfloat16)


def attend_head(queries, cache_keys, cache_values, lengths, new_keys, new_values, reached):
    scale = HEAD ** (-0.5)
    cache_scores = (
        jnp.einsum("bte,ble->btl", queries, cache_keys, preferred_element_type=jnp.float32) * scale
    )
    valid = jnp.arange(cache_keys.shape[1], dtype=jnp.int32)[None, :] < lengths[:, None]
    cache_scores = jnp.where(valid[:, None, :], cache_scores, -jnp.inf)
    draft_scores = (
        jnp.einsum("bte,bse->bts", queries, new_keys, preferred_element_type=jnp.float32) * scale
    )
    draft_scores = jnp.where(reached > 0.5, draft_scores, -jnp.inf)
    highest = jnp.maximum(jnp.max(cache_scores, axis=2), jnp.max(draft_scores, axis=2))
    cache_probs = jnp.exp(cache_scores - highest[..., None])
    draft_probs = jnp.exp(draft_scores - highest[..., None])
    totals = jnp.sum(cache_probs, axis=2) + jnp.sum(draft_probs, axis=2)
    mixed = jnp.einsum(
        "btl,ble->bte",
        cache_probs.astype(jnp.bfloat16),
        cache_values,
        preferred_element_type=jnp.float32,
    )
    mixed = mixed + jnp.einsum(
        "bts,bse->bte",
        draft_probs.astype(jnp.bfloat16),
        new_values,
        preferred_element_type=jnp.float32,
    )
    return (mixed / totals[..., None]).astype(jnp.bfloat16)


def attend(queries, cache_keys, cache_values, lengths, new_keys, new_values, reached):
    parts = []
    for start in range(0, queries.shape[2], HEAD):
        cut = slice(start, start + HEAD)
        parts.append(
            attend_head(
                queries[:, :, cut],
                cache_keys[:, :, cut],
                cache_values[:, :, cut],
                lengths,
                new_keys[:, :, cut],
                new_values[:, :, cut],
                reached,
            )
        )
    return jnp.concatenate(parts, axis=2)


def ring_moves(n_req, n_exp):
    z_size = 4 if n_exp % 4 == 0 else 1
    x_size, y_size = n_exp // z_size, n_req // 2
    order = list(range(0, z_size, 2)) + list(range(1, z_size, 2))[::-1]
    rank = [order.index(z) for z in range(z_size)]

    def along(axis, pairs):
        return lambda value: lax.ppermute(value, axis, pairs)

    def x_pairs(step):
        return [
            (z * x_size + x, z * x_size + (x + step) % x_size)
            for z in range(z_size)
            for x in range(x_size)
        ]

    def y_pairs(step):
        return [
            (y * 2 + c, ((y + step) % y_size) * 2 + c) for y in range(y_size) for c in range(2)
        ]

    z_next = [
        (z * x_size + x, order[(rank[z] + 1) % z_size] * x_size + x)
        for z in range(z_size)
        for x in range(x_size)
    ]
    moves = dict(
        x_on=along("exp", x_pairs(1)),
        x_back=along("exp", x_pairs(-1)),
        y_on=along("req", y_pairs(1)),
        y_back=along("req", y_pairs(-1)),
        z_on=along("exp", z_next),
        swap=along("req", [(r, r ^ 1) for r in range(n_req)]),
    )
    return x_size, y_size, z_size, order, rank, moves


def spread(value, move, size):
    held = [value]
    for step in range(size - 1):
        held.append(move(held[-1]))
    return held


def add16(left, right):
    return (left.astype(jnp.float32) + right.astype(jnp.float32)).astype(jnp.bfloat16)


def collect(terms, move):
    total = terms[-1]
    for term in terms[-2::-1]:
        total = move(total)
        if term is not None:
            total = add16(total, term)
    return total


def plane_gather(block, x_size, y_size, moves):
    half = block.shape[1] // 2
    by_x = spread(block, moves["x_on"], x_size)
    by_y = spread(block, moves["y_on"], y_size)
    left = [spread(by_x[dx][:, :half], moves["y_on"], y_size) for dx in range(1, x_size)]
    right = [spread(by_y[dy][:, half:], moves["x_on"], x_size) for dy in range(1, y_size)]
    rows = []
    for dx in range(x_size):
        for dy in range(y_size):
            if dy == 0:
                rows.append(by_x[dx])
            elif dx == 0:
                rows.append(by_y[dy])
            else:
                rows.append(jnp.concatenate([left[dx - 1][dy], right[dy - 1][dx]], axis=1))
    return jnp.concatenate(rows, axis=0)


def plane_reduce(blocks, x_size, y_size, moves):
    half = blocks.shape[2] // 2
    grid = [[blocks[dx * y_size + dy] for dy in range(y_size)] for dx in range(x_size)]
    by_x, by_y = [None], [None]
    for dx in range(1, x_size):
        left = collect([grid[dx][dy][:, :half] for dy in range(y_size)], moves["y_back"])
        by_x.append(jnp.concatenate([left, grid[dx][0][:, half:]], axis=1))
    for dy in range(1, y_size):
        right = collect([grid[dx][dy][:, half:] for dx in range(x_size)], moves["x_back"])
        by_y.append(jnp.concatenate([grid[0][dy][:, :half], right], axis=1))
    total = grid[0][0].astype(jnp.float32)
    if x_size > 1:
        total = total + collect(by_x, moves["x_back"]).astype(jnp.float32)
    if y_size > 1:
        total = total + collect(by_y, moves["y_back"]).astype(jnp.float32)
    return total


def expert_rows(rows, expert_gate, expert_up, expert_down):
    gate_part = jnp.einsum("snd,sdf->snf", rows, expert_gate, preferred_element_type=jnp.float32)
    up_part = jnp.einsum("snd,sdf->snf", rows, expert_up, preferred_element_type=jnp.float32)
    activation = (jax.nn.silu(gate_part) * up_part).astype(jnp.bfloat16)
    return jnp.einsum("snf,sfd->snd", activation, expert_down, preferred_element_type=jnp.float32)


def route_slots(routes, route_weights):
    tok_rows, top_count = routes.shape
    capacity = 2 * tok_rows * top_count // EXPERTS
    expert_ids = jnp.arange(EXPERTS, dtype=jnp.int32)
    named = jnp.any(routes[:, :, None] == expert_ids[None, None, :], axis=1)
    position = jnp.arange(tok_rows, dtype=jnp.int32)
    earlier = (position[:, None] > position[None, :]).astype(jnp.bfloat16)
    before = jnp.dot(earlier, named.astype(jnp.bfloat16), preferred_element_type=jnp.float32)
    slot = jnp.sum(
        jnp.where(routes[:, :, None] == expert_ids[None, None, :], before[:, None, :], 0.0), axis=2
    )
    target = routes.astype(jnp.float32) * capacity + slot
    return capacity, jnp.concatenate([target.T, route_weights.T], axis=0)


def per_device(
    queries,
    new_keys,
    new_values,
    long_keys,
    long_values,
    long_lengths,
    short_keys,
    short_values,
    short_lengths,
    parents,
    accepted,
    residual,
    out_weight,
    norm_gain,
    routes,
    route_weights,
    expert_gate,
    expert_up,
    expert_down,
):
    n_req, n_exp = lax.axis_size("req"), lax.axis_size("exp")
    req, exp = lax.axis_index("req"), lax.axis_index("exp")
    x_size, y_size, z_size, order, rank, moves = ring_moves(n_req, n_exp)
    z, x, y, core = exp // x_size, exp % x_size, req // 2, req % 2
    me = req * n_exp + exp
    tok_rows, top_count = routes.shape

    capacity, tags = route_slots(routes, route_weights)
    all_tags = lax.all_gather(tags, ("req", "exp"), axis=0, tiled=False)

    half_rows = out_weight.shape[0] // 2
    mine = lax.dynamic_slice_in_dim(out_weight, core * half_rows, half_rows, axis=0)
    weight_mine = lax.all_gather(mine, "exp", axis=0, tiled=False)
    weight_other = moves["swap"](weight_mine)

    reached = ancestors(parents)
    long_out = attend(
        queries[:1], long_keys, long_values, long_lengths, new_keys[:1], new_values[:1], reached[:1]
    )
    short_out = attend(
        queries[1:],
        short_keys,
        short_values,
        short_lengths,
        new_keys[1:],
        new_values[1:],
        reached[1:],
    )
    head_width = new_keys.shape[2]
    attended = jnp.concatenate([long_out, short_out], axis=0).reshape(n_exp, tok_rows, head_width)
    heads_in = lax.all_to_all(attended, "exp", split_axis=0, concat_axis=0, tiled=True)
    heads_mine = lax.dynamic_slice_in_dim(heads_in, core * half_rows, half_rows, axis=2)
    heads_other = lax.dynamic_slice_in_dim(heads_in, (1 - core) * half_rows, half_rows, axis=2)

    def flat_heads(part):
        return jnp.transpose(part, (1, 0, 2)).reshape(tok_rows, -1)

    def flat_weight(part):
        return part.reshape(-1, part.shape[2])

    attn_proj = jnp.dot(
        flat_heads(heads_mine), flat_weight(weight_mine), preferred_element_type=jnp.float32
    ) + jnp.dot(
        flat_heads(heads_other), flat_weight(weight_other), preferred_element_type=jnp.float32
    )
    middle = residual + attn_proj
    normed = (
        middle * lax.rsqrt(jnp.mean(middle * middle, axis=1, keepdims=True) + 1e-05) * norm_gain
    ).astype(jnp.bfloat16)

    slices = expert_gate.shape[0]
    pieces = max(1, n_req * n_exp // EXPERTS)
    first_expert = (me * slices) // pieces
    plane = x_size * y_size
    blocks = 2 * plane
    model_width = normed.shape[1]
    row_count = slices * blocks * capacity
    row_ids = jnp.arange(row_count, dtype=jnp.int32)
    place_of = jnp.arange(blocks, dtype=jnp.int32)

    def chunk_tables(k):
        ring = (jnp.asarray(rank, jnp.int32)[z] - k) % z_size
        far_z = jnp.asarray(order, jnp.int32)[ring]
        owners = []
        for side in range(2):
            owner_core = core if side == 0 else 1 - core
            for dx in range(x_size):
                for dy in range(y_size):
                    owner_req = ((y - dy) % y_size) * 2 + owner_core
                    owners.append(owner_req * n_exp + far_z * x_size + (x - dx) % x_size)
        chosen = all_tags[jnp.stack(owners)]
        target = chosen[:, :top_count].astype(jnp.int32) - first_expert * capacity
        local = (target >= 0) & (target < slices * capacity)
        row = (target // capacity) * (blocks * capacity) + target % capacity
        row = jnp.where(local, row + place_of[:, None, None] * capacity, -1)
        row = jnp.transpose(row, (1, 0, 2)).reshape(top_count, -1)
        weights = jnp.transpose(chosen[:, top_count:], (1, 0, 2)).reshape(top_count, -1)
        hits = row[:, None, :] == row_ids[None, :, None]
        place = jnp.any(hits, axis=0).astype(jnp.bfloat16)
        scale = jnp.sum(jnp.where(hits, weights[:, None, :], 0.0), axis=(0, 2))
        return place, scale

    def chunk_work(tokens, k):
        own = plane_gather(tokens, x_size, y_size, moves)
        other = moves["swap"](own)
        place, scale = chunk_tables(k)
        half_cols = own.shape[0]
        rows = (
            jnp.dot(place[:, :half_cols], own, preferred_element_type=jnp.float32)
            + jnp.dot(place[:, half_cols:], other, preferred_element_type=jnp.float32)
        ).astype(jnp.bfloat16)
        produced = expert_rows(
            rows.reshape(slices, -1, model_width), expert_gate, expert_up, expert_down
        )
        produced = (produced.reshape(row_count, model_width) * scale[:, None]).astype(jnp.bfloat16)
        summed_other = lax.dot_general(
            place[:, half_cols:], produced, (((0,), (0,)), ((), ())), preferred_element_type=jnp.float32
        ).astype(jnp.bfloat16)
        summed_own = lax.dot_general(
            place[:, :half_cols], produced, (((0,), (0,)), ((), ())), preferred_element_type=jnp.float32
        ).astype(jnp.bfloat16)
        both = add16(moves["swap"](summed_other), summed_own)
        return plane_reduce(both.reshape(plane, tok_rows, model_width), x_size, y_size, moves)

    held = spread(normed, moves["z_on"], z_size)
    running = None
    for k in list(range(1, z_size)) + [0]:
        part = chunk_work(held[k], k)
        running = part if running is None else part + running
        if k != 0:
            running = moves["z_on"](running.astype(jnp.bfloat16)).astype(jnp.float32)
    hidden_out = (middle + running).astype(jnp.bfloat16)

    stacked = jnp.concatenate([new_keys, new_values], axis=2)
    compacted = compact_path(reached, accepted, stacked)
    return (hidden_out, compacted[:, :, :head_width], compacted[:, :, head_width:])


def solution(mesh):
    in_specs = (
        P("req", None, "exp"),
        P("req", None, "exp"),
        P("req", None, "exp"),
        P("req", None, "exp"),
        P("req", None, "exp"),
        P("req"),
        P("req", None, "exp"),
        P("req", None, "exp"),
        P("req"),
        P("req", None),
        P("req"),
        P(("req", "exp"), None),
        P("exp", None),
        P(),
        P(("req", "exp"), None),
        P(("req", "exp"), None),
        P(("req", "exp"), None, None),
        P(("req", "exp"), None, None),
        P(("req", "exp"), None, None),
    )
    out_specs = (P(("req", "exp"), None), P("req", None, "exp"), P("req", None, "exp"))
    return jax.shard_map(
        per_device, mesh=mesh, in_specs=in_specs, out_specs=out_specs, check_vma=False
    )
```

```python
import jax
import jax.numpy as jnp
from jax import lax
from jax.sharding import PartitionSpec as P

HEAD = 128
EXPERTS = 64


def ancestors(parents):
    tokens_per = parents.shape[1]
    position = jnp.arange(tokens_per, dtype=jnp.int32)
    identity = position[:, None] == position[None, :]
    linked = (parents[:, :, None] == position[None, None, :]) & (position[None, :, None] > 0)
    reached = (identity[None] | linked).astype(jnp.bfloat16)
    for rounds in range((tokens_per - 1).bit_length()):
        reached = jnp.minimum(
            jnp.einsum("bij,bjk->bik", reached, reached, preferred_element_type=jnp.float32), 1.0
        ).astype(jnp.bfloat16)
    return reached.astype(jnp.float32)


def compact_path(reached, accepted, stacked):
    tokens_per = reached.shape[1]
    position = jnp.arange(tokens_per, dtype=jnp.int32)
    levels = jnp.sum(reached, axis=2) - 1.0
    leaf_row = (accepted[:, None] == position[None, :]).astype(jnp.float32)
    on_path = jnp.sum(leaf_row[:, :, None] * reached, axis=1)
    chooser = on_path[:, None, :] * (
        levels[:, None, :] == position[None, :, None].astype(jnp.float32)
    ).astype(jnp.float32)
    return jnp.einsum(
        "btj,bjc->btc", chooser.astype(jnp.bfloat16), stacked, preferred_element_type=jnp.float32
    ).astype(jnp.bfloat16)


def attend_head(queries, cache_keys, cache_values, lengths, new_keys, new_values, reached):
    scale = HEAD ** (-0.5)
    cache_scores = (
        jnp.einsum("bte,ble->btl", queries, cache_keys, preferred_element_type=jnp.float32) * scale
    )
    valid = jnp.arange(cache_keys.shape[1], dtype=jnp.int32)[None, :] < lengths[:, None]
    cache_scores = jnp.where(valid[:, None, :], cache_scores, -jnp.inf)
    draft_scores = (
        jnp.einsum("bte,bse->bts", queries, new_keys, preferred_element_type=jnp.float32) * scale
    )
    draft_scores = jnp.where(reached > 0.5, draft_scores, -jnp.inf)
    highest = jnp.maximum(jnp.max(cache_scores, axis=2), jnp.max(draft_scores, axis=2))
    cache_probs = jnp.exp(cache_scores - highest[..., None])
    draft_probs = jnp.exp(draft_scores - highest[..., None])
    totals = jnp.sum(cache_probs, axis=2) + jnp.sum(draft_probs, axis=2)
    mixed = jnp.einsum(
        "btl,ble->bte",
        cache_probs.astype(jnp.bfloat16),
        cache_values,
        preferred_element_type=jnp.float32,
    )
    mixed = mixed + jnp.einsum(
        "bts,bse->bte",
        draft_probs.astype(jnp.bfloat16),
        new_values,
        preferred_element_type=jnp.float32,
    )
    return (mixed / totals[..., None]).astype(jnp.bfloat16)


def ring_moves(n_req, n_exp):
    z_size = 4 if n_exp % 4 == 0 else 1
    x_size, y_size = n_exp // z_size, n_req // 2
    order = list(range(0, z_size, 2)) + list(range(1, z_size, 2))[::-1]
    rank = [order.index(z) for z in range(z_size)]

    def along(axis, pairs):
        return lambda value: lax.ppermute(value, axis, pairs)

    def x_pairs(step):
        return [
            (z * x_size + x, z * x_size + (x + step) % x_size)
            for z in range(z_size)
            for x in range(x_size)
        ]

    def y_pairs(step):
        return [
            (y * 2 + c, ((y + step) % y_size) * 2 + c) for y in range(y_size) for c in range(2)
        ]

    z_next = [
        (z * x_size + x, order[(rank[z] + 1) % z_size] * x_size + x)
        for z in range(z_size)
        for x in range(x_size)
    ]
    moves = dict(
        x_on=along("exp", x_pairs(1)),
        x_back=along("exp", x_pairs(-1)),
        y_on=along("req", y_pairs(1)),
        y_back=along("req", y_pairs(-1)),
        z_on=along("exp", z_next),
        swap=along("req", [(r, r ^ 1) for r in range(n_req)]),
    )
    return x_size, y_size, z_size, order, rank, moves


def spread(value, move, size):
    held = [value]
    for step in range(size - 1):
        held.append(move(held[-1]))
    return held


def add16(left, right):
    return (left.astype(jnp.float32) + right.astype(jnp.float32)).astype(jnp.bfloat16)


def collect(terms, move):
    total = terms[-1]
    for term in terms[-2::-1]:
        total = move(total)
        if term is not None:
            total = add16(total, term)
    return total


def plane_gather(block, x_size, y_size, moves):
    half = block.shape[1] // 2
    by_x = spread(block, moves["x_on"], x_size)
    by_y = spread(block, moves["y_on"], y_size)
    left = [spread(by_x[dx][:, :half], moves["y_on"], y_size) for dx in range(1, x_size)]
    right = [spread(by_y[dy][:, half:], moves["x_on"], x_size) for dy in range(1, y_size)]
    rows = []
    for dx in range(x_size):
        for dy in range(y_size):
            if dy == 0:
                rows.append(by_x[dx])
            elif dx == 0:
                rows.append(by_y[dy])
            else:
                rows.append(jnp.concatenate([left[dx - 1][dy], right[dy - 1][dx]], axis=1))
    return jnp.concatenate(rows, axis=0)


def plane_reduce(blocks, x_size, y_size, moves):
    half = blocks.shape[2] // 2
    grid = [[blocks[dx * y_size + dy] for dy in range(y_size)] for dx in range(x_size)]
    by_x, by_y = [None], [None]
    for dx in range(1, x_size):
        left = collect([grid[dx][dy][:, :half] for dy in range(y_size)], moves["y_back"])
        by_x.append(jnp.concatenate([left, grid[dx][0][:, half:]], axis=1))
    for dy in range(1, y_size):
        right = collect([grid[dx][dy][:, half:] for dx in range(x_size)], moves["x_back"])
        by_y.append(jnp.concatenate([grid[0][dy][:, :half], right], axis=1))
    total = grid[0][0].astype(jnp.float32)
    if x_size > 1:
        total = total + collect(by_x, moves["x_back"]).astype(jnp.float32)
    if y_size > 1:
        total = total + collect(by_y, moves["y_back"]).astype(jnp.float32)
    return total


def expert_rows(rows, expert_gate, expert_up, expert_down):
    gate_part = jnp.einsum("snd,sdf->snf", rows, expert_gate, preferred_element_type=jnp.float32)
    up_part = jnp.einsum("snd,sdf->snf", rows, expert_up, preferred_element_type=jnp.float32)
    gate_part, up_part = lax.optimization_barrier((gate_part, up_part))
    activation = lax.optimization_barrier((jax.nn.silu(gate_part) * up_part).astype(jnp.bfloat16))
    return jnp.einsum("snf,sfd->snd", activation, expert_down, preferred_element_type=jnp.float32)


def route_slots(routes, route_weights):
    tok_rows, top_count = routes.shape
    capacity = 2 * tok_rows * top_count // EXPERTS
    expert_ids = jnp.arange(EXPERTS, dtype=jnp.int32)
    named = jnp.any(routes[:, :, None] == expert_ids[None, None, :], axis=1)
    position = jnp.arange(tok_rows, dtype=jnp.int32)
    earlier = (position[:, None] > position[None, :]).astype(jnp.bfloat16)
    before = jnp.dot(earlier, named.astype(jnp.bfloat16), preferred_element_type=jnp.float32)
    slot = jnp.sum(
        jnp.where(routes[:, :, None] == expert_ids[None, None, :], before[:, None, :], 0.0), axis=2
    )
    target = routes.astype(jnp.float32) * capacity + slot
    return capacity, jnp.concatenate([target.T, route_weights.T], axis=0)


def per_device(
    queries,
    new_keys,
    new_values,
    long_keys,
    long_values,
    long_lengths,
    short_keys,
    short_values,
    short_lengths,
    parents,
    accepted,
    residual,
    out_weight,
    norm_gain,
    routes,
    route_weights,
    expert_gate,
    expert_up,
    expert_down,
):
    n_req, n_exp = lax.axis_size("req"), lax.axis_size("exp")
    req, exp = lax.axis_index("req"), lax.axis_index("exp")
    x_size, y_size, z_size, order, rank, moves = ring_moves(n_req, n_exp)
    z, x, y, core = exp // x_size, exp % x_size, req // 2, req % 2
    me = req * n_exp + exp
    tok_rows, top_count = routes.shape

    capacity, tags = route_slots(routes, route_weights)
    share = out_weight.shape[0] // n_req
    mine = lax.dynamic_slice_in_dim(out_weight, req * share, share, axis=0)
    reached = ancestors(parents)
    head_width = new_keys.shape[2]
    short_ones = (short_keys, short_values, short_lengths, 1, reached.shape[0])
    long_ones = (long_keys, long_values, long_lengths, 0, 1)
    jobs = [(group, h) for group in (short_ones, long_ones) for h in range(0, head_width, HEAD)]

    def tag_step(step, tags):
        if step == 0:
            tags = jnp.stack([tags, moves["swap"](tags)])
            return jnp.stack(spread(tags, moves["y_on"], y_size), axis=1)
        if step == 1:
            return jnp.stack(spread(tags, moves["x_on"], x_size), axis=1)
        return tags

    outs, weights = [], []
    for step, ((keys, values, lengths, low, high), h) in enumerate(jobs):
        asked = queries[low:high, :, h : h + HEAD]
        if step > 0:
            asked, mine, weights[-1], tags = lax.optimization_barrier(
                (asked, mine, weights[-1], tags)
            )
        outs.append(
            attend_head(
                asked,
                keys[:, :, h : h + HEAD],
                values[:, :, h : h + HEAD],
                lengths,
                new_keys[low:high, :, h : h + HEAD],
                new_values[low:high, :, h : h + HEAD],
                reached[low:high],
            )
        )
        if step < z_size:
            weights.append(plane_gather(mine, x_size, y_size, moves))
            tags = tag_step(step, tags)
            if step < z_size - 1:
                mine = moves["z_on"](mine)
    for step in range(len(jobs), z_size):
        weights.append(plane_gather(mine, x_size, y_size, moves))
        tags = tag_step(step, tags)
        if step < z_size - 1:
            mine = moves["z_on"](mine)
    weights = [part for one in weights for part in (one, moves["swap"](one))]
    all_tags = [part.reshape(-1, 2 * top_count, tok_rows) for part in spread(tags, moves["z_on"], z_size)]
    count = len(outs) // 2
    short_out = jnp.concatenate(outs[:count], axis=2)
    long_out = jnp.concatenate(outs[count:], axis=2)
    attended = jnp.concatenate([long_out, short_out], axis=0).reshape(n_exp, tok_rows, head_width)
    heads_in = lax.all_to_all(attended, "exp", split_axis=0, concat_axis=0, tiled=True)
    heads = jnp.transpose(heads_in.reshape(n_exp, tok_rows, n_req, share), (0, 2, 1, 3))
    heads = heads.reshape(n_exp * n_req, tok_rows, share)
    sources = []
    for k in range(z_size):
        far_z = jnp.asarray(order, jnp.int32)[(jnp.asarray(rank, jnp.int32)[z] - k) % z_size]
        for side in range(2):
            from_core = core if side == 0 else 1 - core
            for dx in range(x_size):
                for dy in range(y_size):
                    from_req = ((y - dy) % y_size) * 2 + from_core
                    sources.append((far_z * x_size + (x - dx) % x_size) * n_req + from_req)
    picks = jnp.stack(sources)[:, None] == jnp.arange(n_exp * n_req, dtype=jnp.int32)[None, :]
    heads = jnp.einsum(
        "ij,jtc->itc", picks.astype(jnp.bfloat16), heads, preferred_element_type=jnp.float32
    ).astype(jnp.bfloat16)
    group = x_size * y_size
    attn_proj = 0.0
    for place, weight in enumerate(weights):
        part = jnp.transpose(heads[place * group : (place + 1) * group], (1, 0, 2))
        attn_proj = attn_proj + jnp.dot(
            part.reshape(tok_rows, -1), weight, preferred_element_type=jnp.float32
        )
    middle = residual + attn_proj
    normed = (
        middle * lax.rsqrt(jnp.mean(middle * middle, axis=1, keepdims=True) + 1e-05) * norm_gain
    ).astype(jnp.bfloat16)

    slices = expert_gate.shape[0]
    pieces = max(1, n_req * n_exp // EXPERTS)
    first_expert = (me * slices) // pieces
    plane = x_size * y_size
    blocks = 2 * plane
    model_width = normed.shape[1]
    row_count = slices * blocks * capacity
    row_ids = jnp.arange(row_count, dtype=jnp.int32)
    place_of = jnp.arange(blocks, dtype=jnp.int32)

    def chunk_tables(k):
        chosen = all_tags[k]
        target = chosen[:, :top_count].astype(jnp.int32) - first_expert * capacity
        local = (target >= 0) & (target < slices * capacity)
        row = (target // capacity) * (blocks * capacity) + target % capacity
        row = jnp.where(local, row + place_of[:, None, None] * capacity, -1)
        row = jnp.transpose(row, (1, 0, 2)).reshape(top_count, -1)
        weights = jnp.transpose(chosen[:, top_count:], (1, 0, 2)).reshape(top_count, -1)
        hits = row[:, None, :] == row_ids[None, :, None]
        place = jnp.any(hits, axis=0).astype(jnp.bfloat16)
        scale = jnp.sum(jnp.where(hits, weights[:, None, :], 0.0), axis=(0, 2))
        return place, scale

    def chunk_gather(tokens):
        own = plane_gather(tokens, x_size, y_size, moves)
        return own, moves["swap"](own)

    def chunk_work(own, other, k):
        place, scale = chunk_tables(k)
        half_cols = own.shape[0]
        rows = (
            jnp.dot(place[:, :half_cols], own, preferred_element_type=jnp.float32)
            + jnp.dot(place[:, half_cols:], other, preferred_element_type=jnp.float32)
        ).astype(jnp.bfloat16)
        produced = expert_rows(
            rows.reshape(slices, -1, model_width), expert_gate, expert_up, expert_down
        )
        produced = (produced.reshape(row_count, model_width) * scale[:, None]).astype(jnp.bfloat16)
        summed_other = lax.dot_general(
            place[:, half_cols:], produced, (((0,), (0,)), ((), ())), preferred_element_type=jnp.float32
        ).astype(jnp.bfloat16)
        summed_own = lax.dot_general(
            place[:, :half_cols], produced, (((0,), (0,)), ((), ())), preferred_element_type=jnp.float32
        ).astype(jnp.bfloat16)
        both = add16(moves["swap"](summed_other), summed_own)
        reduced = plane_reduce(both.reshape(plane, tok_rows, model_width), x_size, y_size, moves)
        return rows, both, reduced

    held = spread(normed, moves["z_on"], z_size)
    running = None
    steps = list(range(1, z_size)) + [0]
    started, summed = [], []
    for step, k in enumerate(steps):
        tokens = held[k]
        if step >= 2:
            tokens, started[step - 2] = lax.optimization_barrier((tokens, started[step - 2]))
        own, other = chunk_gather(tokens)
        if step >= 2:
            own, other, summed[step - 2] = lax.optimization_barrier((own, other, summed[step - 2]))
        rows, both, part = chunk_work(own, other, k)
        started.append(rows)
        summed.append(both)
        running = part if running is None else part + running
        if k != 0:
            running = moves["z_on"](running.astype(jnp.bfloat16)).astype(jnp.float32)
    hidden_out = (middle + running).astype(jnp.bfloat16)

    stacked = jnp.concatenate([new_keys, new_values], axis=2)
    compacted = compact_path(reached, accepted, stacked)
    return (hidden_out, compacted[:, :, :head_width], compacted[:, :, head_width:])


def solution(mesh):
    in_specs = (
        P("req", None, "exp"),
        P("req", None, "exp"),
        P("req", None, "exp"),
        P("req", None, "exp"),
        P("req", None, "exp"),
        P("req"),
        P("req", None, "exp"),
        P("req", None, "exp"),
        P("req"),
        P("req", None),
        P("req"),
        P(("req", "exp"), None),
        P("exp", None),
        P(),
        P(("req", "exp"), None),
        P(("req", "exp"), None),
        P(("req", "exp"), None, None),
        P(("req", "exp"), None, None),
        P(("req", "exp"), None, None),
    )
    out_specs = (P(("req", "exp"), None), P("req", None, "exp"), P("req", None, "exp"))
    return jax.shard_map(
        per_device, mesh=mesh, in_specs=in_specs, out_specs=out_specs, check_vma=False
    )
```

```python
import jax
import jax.numpy as jnp
from jax import lax
from jax.sharding import PartitionSpec as P

HEAD = 128
EXPERTS = 64


def ancestors(parents):
    tokens_per = parents.shape[1]
    position = jnp.arange(tokens_per, dtype=jnp.int32)
    identity = position[:, None] == position[None, :]
    linked = (parents[:, :, None] == position[None, None, :]) & (position[None, :, None] > 0)
    reached = (identity[None] | linked).astype(jnp.bfloat16)
    for rounds in range((tokens_per - 1).bit_length()):
        reached = jnp.minimum(
            jnp.einsum("bij,bjk->bik", reached, reached, preferred_element_type=jnp.float32), 1.0
        ).astype(jnp.bfloat16)
    return reached.astype(jnp.float32)


def compact_path(reached, accepted, stacked):
    tokens_per = reached.shape[1]
    position = jnp.arange(tokens_per, dtype=jnp.int32)
    levels = jnp.sum(reached, axis=2) - 1.0
    leaf_row = (accepted[:, None] == position[None, :]).astype(jnp.float32)
    on_path = jnp.sum(leaf_row[:, :, None] * reached, axis=1)
    chooser = on_path[:, None, :] * (
        levels[:, None, :] == position[None, :, None].astype(jnp.float32)
    ).astype(jnp.float32)
    return jnp.einsum(
        "btj,bjc->btc", chooser.astype(jnp.bfloat16), stacked, preferred_element_type=jnp.float32
    ).astype(jnp.bfloat16)


def attend_head(queries, cache_keys, cache_values, lengths, new_keys, new_values, reached):
    scale = HEAD ** (-0.5)
    cache_scores = (
        jnp.einsum("bte,ble->btl", queries, cache_keys, preferred_element_type=jnp.float32) * scale
    )
    valid = jnp.arange(cache_keys.shape[1], dtype=jnp.int32)[None, :] < lengths[:, None]
    cache_scores = jnp.where(valid[:, None, :], cache_scores, -jnp.inf)
    draft_scores = (
        jnp.einsum("bte,bse->bts", queries, new_keys, preferred_element_type=jnp.float32) * scale
    )
    draft_scores = jnp.where(reached > 0.5, draft_scores, -jnp.inf)
    highest = jnp.maximum(jnp.max(cache_scores, axis=2), jnp.max(draft_scores, axis=2))
    cache_probs = jnp.exp(cache_scores - highest[..., None])
    draft_probs = jnp.exp(draft_scores - highest[..., None])
    totals = jnp.sum(cache_probs, axis=2) + jnp.sum(draft_probs, axis=2)
    mixed = jnp.einsum(
        "btl,ble->bte",
        cache_probs.astype(jnp.bfloat16),
        cache_values,
        preferred_element_type=jnp.float32,
    )
    mixed = mixed + jnp.einsum(
        "bts,bse->bte",
        draft_probs.astype(jnp.bfloat16),
        new_values,
        preferred_element_type=jnp.float32,
    )
    return (mixed / totals[..., None]).astype(jnp.bfloat16)


def ring_moves(n_req, n_exp):
    z_size = 4 if n_exp % 4 == 0 else 1
    x_size, y_size = n_exp // z_size, n_req // 2
    order = list(range(0, z_size, 2)) + list(range(1, z_size, 2))[::-1]
    rank = [order.index(z) for z in range(z_size)]

    def along(axis, pairs):
        return lambda value: lax.ppermute(value, axis, pairs)

    def x_pairs(step):
        return [
            (z * x_size + x, z * x_size + (x + step) % x_size)
            for z in range(z_size)
            for x in range(x_size)
        ]

    def y_pairs(step):
        return [
            (y * 2 + c, ((y + step) % y_size) * 2 + c) for y in range(y_size) for c in range(2)
        ]

    z_next = [
        (z * x_size + x, order[(rank[z] + 1) % z_size] * x_size + x)
        for z in range(z_size)
        for x in range(x_size)
    ]
    moves = dict(
        x_on=along("exp", x_pairs(1)),
        x_back=along("exp", x_pairs(-1)),
        y_on=along("req", y_pairs(1)),
        y_back=along("req", y_pairs(-1)),
        z_on=along("exp", z_next),
        swap=along("req", [(r, r ^ 1) for r in range(n_req)]),
    )
    return x_size, y_size, z_size, order, rank, moves


def spread(value, move, size):
    held = [value]
    for step in range(size - 1):
        held.append(move(held[-1]))
    return held


def add16(left, right):
    return (left.astype(jnp.float32) + right.astype(jnp.float32)).astype(jnp.bfloat16)


def collect(terms, move):
    total = terms[-1]
    for term in terms[-2::-1]:
        total = move(total)
        if term is not None:
            total = add16(total, term)
    return total


def plane_gather(block, x_size, y_size, moves):
    half = block.shape[1] // 2
    by_x = spread(block, moves["x_on"], x_size)
    by_y = spread(block, moves["y_on"], y_size)
    left = [spread(by_x[dx][:, :half], moves["y_on"], y_size) for dx in range(1, x_size)]
    right = [spread(by_y[dy][:, half:], moves["x_on"], x_size) for dy in range(1, y_size)]
    rows = []
    for dx in range(x_size):
        for dy in range(y_size):
            if dy == 0:
                rows.append(by_x[dx])
            elif dx == 0:
                rows.append(by_y[dy])
            else:
                rows.append(jnp.concatenate([left[dx - 1][dy], right[dy - 1][dx]], axis=1))
    return jnp.concatenate(rows, axis=0)


def plane_reduce(blocks, x_size, y_size, moves):
    half = blocks.shape[2] // 2
    grid = [[blocks[dx * y_size + dy] for dy in range(y_size)] for dx in range(x_size)]
    by_x, by_y = [None], [None]
    for dx in range(1, x_size):
        left = collect([grid[dx][dy][:, :half] for dy in range(y_size)], moves["y_back"])
        by_x.append(jnp.concatenate([left, grid[dx][0][:, half:]], axis=1))
    for dy in range(1, y_size):
        right = collect([grid[dx][dy][:, half:] for dx in range(x_size)], moves["x_back"])
        by_y.append(jnp.concatenate([grid[0][dy][:, :half], right], axis=1))
    total = grid[0][0].astype(jnp.float32)
    if x_size > 1:
        total = total + collect(by_x, moves["x_back"]).astype(jnp.float32)
    if y_size > 1:
        total = total + collect(by_y, moves["y_back"]).astype(jnp.float32)
    return total


def expert_rows(rows, expert_gate, expert_up, expert_down):
    gate_part = jnp.einsum("snd,sdf->snf", rows, expert_gate, preferred_element_type=jnp.float32)
    up_part = jnp.einsum("snd,sdf->snf", rows, expert_up, preferred_element_type=jnp.float32)
    gate_part, up_part = lax.optimization_barrier((gate_part, up_part))
    activation = lax.optimization_barrier((jax.nn.silu(gate_part) * up_part).astype(jnp.bfloat16))
    return jnp.einsum("snf,sfd->snd", activation, expert_down, preferred_element_type=jnp.float32)


def route_slots(routes, route_weights):
    tok_rows, top_count = routes.shape
    capacity = 2 * tok_rows * top_count // EXPERTS
    expert_ids = jnp.arange(EXPERTS, dtype=jnp.int32)
    named = jnp.any(routes[:, :, None] == expert_ids[None, None, :], axis=1)
    position = jnp.arange(tok_rows, dtype=jnp.int32)
    earlier = (position[:, None] > position[None, :]).astype(jnp.bfloat16)
    before = jnp.dot(earlier, named.astype(jnp.bfloat16), preferred_element_type=jnp.float32)
    slot = jnp.sum(
        jnp.where(routes[:, :, None] == expert_ids[None, None, :], before[:, None, :], 0.0), axis=2
    )
    target = routes.astype(jnp.float32) * capacity + slot
    return capacity, jnp.concatenate([target.T, route_weights.T], axis=0)


def per_device(
    queries,
    new_keys,
    new_values,
    long_keys,
    long_values,
    long_lengths,
    short_keys,
    short_values,
    short_lengths,
    parents,
    accepted,
    residual,
    out_weight,
    norm_gain,
    routes,
    route_weights,
    expert_gate,
    expert_up,
    expert_down,
):
    n_req, n_exp = lax.axis_size("req"), lax.axis_size("exp")
    req, exp = lax.axis_index("req"), lax.axis_index("exp")
    x_size, y_size, z_size, order, rank, moves = ring_moves(n_req, n_exp)
    z, x, y, core = exp // x_size, exp % x_size, req // 2, req % 2
    me = req * n_exp + exp
    tok_rows, top_count = routes.shape

    capacity, tags = route_slots(routes, route_weights)
    share = out_weight.shape[0] // n_req
    mine = lax.dynamic_slice_in_dim(out_weight, req * share, share, axis=0)
    reached = ancestors(parents)
    head_width = new_keys.shape[2]
    short_ones = (short_keys, short_values, short_lengths, 1, reached.shape[0])
    long_ones = (long_keys, long_values, long_lengths, 0, 1)
    jobs = [(group, h) for group in (short_ones, long_ones) for h in range(0, head_width, HEAD)]

    def tag_step(step, tags):
        if step == 0:
            tags = jnp.stack([tags, moves["swap"](tags)])
            return jnp.stack(spread(tags, moves["y_on"], y_size), axis=1)
        if step == 1:
            return jnp.stack(spread(tags, moves["x_on"], x_size), axis=1)
        if step == 2:
            return jnp.stack(spread(tags, moves["z_on"], z_size))
        return tags

    outs, weights = [], []
    for step, ((keys, values, lengths, low, high), h) in enumerate(jobs):
        asked = queries[low:high, :, h : h + HEAD]
        if step > 0:
            asked, mine, weights[-1], tags = lax.optimization_barrier(
                (asked, mine, weights[-1], tags)
            )
        outs.append(
            attend_head(
                asked,
                keys[:, :, h : h + HEAD],
                values[:, :, h : h + HEAD],
                lengths,
                new_keys[low:high, :, h : h + HEAD],
                new_values[low:high, :, h : h + HEAD],
                reached[low:high],
            )
        )
        if step < z_size:
            weights.append(plane_gather(mine, x_size, y_size, moves))
            tags = tag_step(step, tags)
            if step < z_size - 1:
                mine = moves["z_on"](mine)
    for step in range(len(jobs), z_size):
        weights.append(plane_gather(mine, x_size, y_size, moves))
        tags = tag_step(step, tags)
        if step < z_size - 1:
            mine = moves["z_on"](mine)
    weights = [part for one in weights for part in (one, moves["swap"](one))]
    all_tags = [tags[k].reshape(-1, 2 * top_count, tok_rows) for k in range(z_size)]
    count = len(outs) // 2
    short_out = jnp.concatenate(outs[:count], axis=2)
    long_out = jnp.concatenate(outs[count:], axis=2)
    attended = jnp.concatenate([long_out, short_out], axis=0).reshape(n_exp, tok_rows, head_width)
    heads_in = lax.all_to_all(attended, "exp", split_axis=0, concat_axis=0, tiled=True)
    heads = jnp.transpose(heads_in.reshape(n_exp, tok_rows, n_req, share), (0, 2, 1, 3))
    heads = heads.reshape(n_exp * n_req, tok_rows, share)
    sources = []
    for k in range(z_size):
        far_z = jnp.asarray(order, jnp.int32)[(jnp.asarray(rank, jnp.int32)[z] - k) % z_size]
        for side in range(2):
            from_core = core if side == 0 else 1 - core
            for dx in range(x_size):
                for dy in range(y_size):
                    from_req = ((y - dy) % y_size) * 2 + from_core
                    sources.append((far_z * x_size + (x - dx) % x_size) * n_req + from_req)
    picks = jnp.stack(sources)[:, None] == jnp.arange(n_exp * n_req, dtype=jnp.int32)[None, :]
    heads = jnp.einsum(
        "ij,jtc->itc", picks.astype(jnp.bfloat16), heads, preferred_element_type=jnp.float32
    ).astype(jnp.bfloat16)
    group = x_size * y_size
    attn_proj = 0.0
    for place, weight in enumerate(weights):
        part = jnp.transpose(heads[place * group : (place + 1) * group], (1, 0, 2))
        attn_proj = attn_proj + jnp.dot(
            part.reshape(tok_rows, -1), weight, preferred_element_type=jnp.float32
        )
    middle = residual + attn_proj
    normed = (
        middle * lax.rsqrt(jnp.mean(middle * middle, axis=1, keepdims=True) + 1e-05) * norm_gain
    ).astype(jnp.bfloat16)

    slices = expert_gate.shape[0]
    pieces = max(1, n_req * n_exp // EXPERTS)
    first_expert = (me * slices) // pieces
    plane = x_size * y_size
    blocks = 2 * plane
    model_width = normed.shape[1]
    row_count = slices * blocks * capacity
    row_ids = jnp.arange(row_count, dtype=jnp.int32)
    place_of = jnp.arange(blocks, dtype=jnp.int32)

    def chunk_tables(k):
        chosen = all_tags[k]
        target = chosen[:, :top_count].astype(jnp.int32) - first_expert * capacity
        local = (target >= 0) & (target < slices * capacity)
        row = (target // capacity) * (blocks * capacity) + target % capacity
        row = jnp.where(local, row + place_of[:, None, None] * capacity, -1)
        row = jnp.transpose(row, (1, 0, 2)).reshape(top_count, -1)
        weights = jnp.transpose(chosen[:, top_count:], (1, 0, 2)).reshape(top_count, -1)
        hits = row[:, None, :] == row_ids[None, :, None]
        place = jnp.any(hits, axis=0).astype(jnp.bfloat16)
        scale = jnp.sum(jnp.where(hits, weights[:, None, :], 0.0), axis=(0, 2))
        return place, scale

    def chunk_gather(tokens):
        own = plane_gather(tokens, x_size, y_size, moves)
        return own, moves["swap"](own)

    def chunk_work(own, other, k):
        place, scale = chunk_tables(k)
        half_cols = own.shape[0]
        rows = (
            jnp.dot(place[:, :half_cols], own, preferred_element_type=jnp.float32)
            + jnp.dot(place[:, half_cols:], other, preferred_element_type=jnp.float32)
        ).astype(jnp.bfloat16)
        produced = expert_rows(
            rows.reshape(slices, -1, model_width), expert_gate, expert_up, expert_down
        )
        produced = (produced.reshape(row_count, model_width) * scale[:, None]).astype(jnp.bfloat16)
        summed_other = lax.dot_general(
            place[:, half_cols:], produced, (((0,), (0,)), ((), ())), preferred_element_type=jnp.float32
        ).astype(jnp.bfloat16)
        summed_own = lax.dot_general(
            place[:, :half_cols], produced, (((0,), (0,)), ((), ())), preferred_element_type=jnp.float32
        ).astype(jnp.bfloat16)
        both = add16(moves["swap"](summed_other), summed_own)
        reduced = plane_reduce(both.reshape(plane, tok_rows, model_width), x_size, y_size, moves)
        return rows, both, reduced

    held = spread(normed, moves["z_on"], z_size)
    running = None
    steps = list(range(1, z_size)) + [0]
    started, summed = [], []
    for step, k in enumerate(steps):
        tokens = held[k]
        if step >= 2:
            tokens, started[step - 2] = lax.optimization_barrier((tokens, started[step - 2]))
        own, other = chunk_gather(tokens)
        if step >= 2:
            own, other, summed[step - 2] = lax.optimization_barrier((own, other, summed[step - 2]))
        rows, both, part = chunk_work(own, other, k)
        started.append(rows)
        summed.append(both)
        running = part if running is None else part + running
        if k != 0:
            running = moves["z_on"](running.astype(jnp.bfloat16)).astype(jnp.float32)
    hidden_out = (middle + running).astype(jnp.bfloat16)

    stacked = jnp.concatenate([new_keys, new_values], axis=2)
    compacted = compact_path(reached, accepted, stacked)
    return (hidden_out, compacted[:, :, :head_width], compacted[:, :, head_width:])


def solution(mesh):
    in_specs = (
        P("req", None, "exp"),
        P("req", None, "exp"),
        P("req", None, "exp"),
        P("req", None, "exp"),
        P("req", None, "exp"),
        P("req"),
        P("req", None, "exp"),
        P("req", None, "exp"),
        P("req"),
        P("req", None),
        P("req"),
        P(("req", "exp"), None),
        P("exp", None),
        P(),
        P(("req", "exp"), None),
        P(("req", "exp"), None),
        P(("req", "exp"), None, None),
        P(("req", "exp"), None, None),
        P(("req", "exp"), None, None),
    )
    out_specs = (P(("req", "exp"), None), P("req", None, "exp"), P("req", None, "exp"))
    return jax.shard_map(
        per_device, mesh=mesh, in_specs=in_specs, out_specs=out_specs, check_vma=False
    )
```
